512 devices in a mesh: ctx: 64 (over y, z), head: 8 (over x, core).
Axes of the slice: x: 4, y: 8, z: 8, core: 2. Of those that a mesh axis runs over, the one named last changes fastest.
Arguments:
- queries: bfloat16 [8192, 4096], P('ctx', 'head'), may hold values from -6 to 6
- keys: bfloat16 [8192, 4096], P('ctx', 'head'), may hold values from -6 to 6
- values: bfloat16 [8192, 4096], P('ctx', 'head'), may hold values from -6 to 6
- out_weight: bfloat16 [4096, 4096], P('head', 'ctx'), may hold values from -0.25 to 0.25
- grad_out: bfloat16 [8192, 4096], P('ctx', 'head'), may hold values from -6 to 6
Outputs:
- mixed: bfloat16 [8192, 4096], P('ctx', 'head')
- grad_queries: bfloat16 [8192, 4096], P('ctx', 'head')
- grad_keys: bfloat16 [8192, 4096], P('ctx', 'head')
- grad_values: bfloat16 [8192, 4096], P('ctx', 'head')
The draws below stay inside these ranges and needn't reach their ends.
All inputs are finite; a program needn't handle non-finite values.
Results may differ from the reference program's by a relative error of at most 0.017.
Values may be sent and summed in bfloat16 or wider, within the bound.
No kernel may reach another device: no remote copies, remote signals or barrier semaphores. Data moves between devices by JAX's collectives and lax.ppermute only.
A program may use at most 64 MiB of HBM per device.

```python
import jax
import jax.numpy as jnp
from jax import lax

D = 4096
HEAD_DIM = 128
TOK_DEV = 128
HEADS = 32
TOKENS = 8192
N_HEAD = 8


def raised(drawn, own_key, source, target, blocks, factor):
    def block_of(position):
        return (jnp.arange(drawn.shape[position]) // (drawn.shape[position] // blocks)).reshape((-1,) + (1,) * (drawn.ndim - 1 - position))

    one_side = jax.random.permutation(own_key, blocks)[block_of(target)]
    far = (block_of(target) + blocks // 2) % blocks
    return jnp.where((block_of(source) == one_side) | (block_of(source) == far), factor * drawn, drawn)


def shard_levels(stream_key, shape, shards, smallest, high):
    loudness = 1.0
    for dim, blocks in shards:
        draws = jax.random.uniform(jax.random.fold_in(jax.random.fold_in(stream_key, 6), dim), (blocks,), jnp.float32, smallest / len(shards), high / len(shards))
        loudness = loudness * jnp.repeat(jnp.exp(draws), shape[dim] // blocks).reshape((-1,) + (1,) * (len(shape) - 1 - dim))
    return loudness


def normal_values(stream_key, dims, spread, reach, split=(), held_as=jnp.bfloat16):
    array = spread * jax.random.normal(stream_key, dims, jnp.float32)
    if split:
        array = array * shard_levels(stream_key, dims, split, -0.22, 0.18)
    return jnp.clip(array, -reach, reach).astype(held_as)


def bell_draw_with(own_key, extent, deviation, reach, cuts, heavy, kind=jnp.bfloat16):
    result = deviation * jax.random.normal(own_key, extent, jnp.float32)
    if cuts:
        result = result * shard_levels(own_key, extent, cuts, -0.22, 0.18)
    return jnp.clip(raised(result, jax.random.fold_in(own_key, 3), *heavy), -reach, reach).astype(kind)


def setup_inputs(seed: int = 0) -> dict:
    streams_of = jax.random.split(jax.random.key(seed), 6)
    queries = normal_values(streams_of[0], (TOKENS, HEADS * HEAD_DIM), 1.0, 6.0, ((0, 64), (1, 8)))
    keys = normal_values(streams_of[1], (TOKENS, HEADS * HEAD_DIM), 1.0, 6.0, ((0, 64), (1, 8)))
    values = normal_values(streams_of[2], (TOKENS, HEADS * HEAD_DIM), 1.0, 6.0, ((0, 64), (1, 8)))
    out_weight = bell_draw_with(streams_of[3], (HEADS * HEAD_DIM, D), (HEADS * HEAD_DIM) ** -0.5, 0.25, ((0, 8), (1, 64)), (0, 1, 64, 4.0))
    grad_out = normal_values(streams_of[4], (TOKENS, D), 1.0, 6.0, ((0, 64), (1, 8)))
    return {"queries": queries, "keys": keys, "values": values, "out_weight": out_weight, "grad_out": grad_out}


epsilon = 1e-06

def rounded(matrix):
    return lax.optimization_barrier(matrix.astype(jnp.bfloat16)).astype(jnp.float32)

def split_heads(matrix, blocks):
    return matrix.reshape(blocks, TOK_DEV, matrix.shape[1] // HEAD_DIM, HEAD_DIM)

def reference(queries, keys, values, out_weight, grad_out):
    length = queries.shape[0]
    blocks = length // TOK_DEV
    heads = queries.shape[1] // HEAD_DIM
    causal = jnp.tril(jnp.ones((TOK_DEV, TOK_DEV), dtype=bool))[None]
    highest = lax.Precision.HIGHEST
    query_blocks = split_heads(queries, blocks)
    key_blocks = split_heads(keys, blocks)
    value_blocks = split_heads(values, blocks)

    def forward_block(state, pieces):
        query_part = pieces[0].astype(jnp.float32)
        key_part = pieces[1].astype(jnp.float32)
        value_part = pieces[2].astype(jnp.float32)
        scores = jnp.einsum('ihe,jhe->hij', query_part, key_part)
        attn_weights = rounded(jnp.where(causal, scores, 0.0))
        within = jnp.einsum('hij,jhe->ihe', attn_weights, value_part)
        carried = jnp.einsum('ihd,hde->ihe', query_part, state, precision=highest)
        grown = state + jnp.einsum('ihd,ihe->hde', key_part, value_part)
        return (grown, (within + carried, state))
    start_state = jnp.zeros((heads, HEAD_DIM, HEAD_DIM), jnp.float32)
    final_state, (attended, prefixes) = lax.scan(forward_block, start_state, (query_blocks, key_blocks, value_blocks))
    scale_rows = lax.rsqrt(lax.optimization_barrier(jnp.mean(attended * attended, axis=-1, keepdims=True)) + epsilon)
    normed = attended * scale_rows
    flat_normed = normed.astype(jnp.bfloat16).reshape(length, heads * HEAD_DIM)
    grouped_weight = out_weight.reshape(N_HEAD, out_weight.shape[0] // N_HEAD, out_weight.shape[1]).astype(jnp.float32)

    def project_block(rows):
        grouped_rows = rows.reshape(TOK_DEV, N_HEAD, -1).astype(jnp.float32)
        partials = jnp.einsum('bgc,gcd->gbd', grouped_rows, grouped_weight)
        return lax.optimization_barrier(jnp.sum(rounded(partials), axis=0)).astype(jnp.bfloat16)
    mixed = lax.map(project_block, flat_normed.reshape(blocks, TOK_DEV, -1)).reshape(length, -1)
    grad_normed = jnp.dot(grad_out, out_weight.T, preferred_element_type=jnp.float32)
    grad_normed = grad_normed.reshape(blocks, TOK_DEV, heads, HEAD_DIM)
    grad_attended = scale_rows * (grad_normed - normed * lax.optimization_barrier(jnp.mean(grad_normed * normed, axis=-1, keepdims=True)))
    grad_blocks = grad_attended.astype(jnp.bfloat16)

    def backward_block(state, pieces):
        query_part = pieces[0].astype(jnp.float32)
        key_part = pieces[1].astype(jnp.float32)
        value_part = pieces[2].astype(jnp.float32)
        grad_part = pieces[3].astype(jnp.float32)
        before = pieces[4]
        scores = jnp.einsum('ihe,jhe->hij', query_part, key_part)
        attn_weights = rounded(jnp.where(causal, scores, 0.0))
        grad_scores = rounded(jnp.where(causal, jnp.einsum('ihe,jhe->hij', grad_part, value_part), 0.0))
        grad_query = jnp.einsum('hij,jhd->ihd', grad_scores, key_part) + jnp.einsum('ihe,hde->ihd', grad_part, before, precision=highest)
        grad_key = jnp.einsum('hij,ihd->jhd', grad_scores, query_part) + jnp.einsum('jhe,hde->jhd', value_part, state, precision=highest)
        grad_value = jnp.einsum('hij,ihe->jhe', attn_weights, grad_part) + jnp.einsum('jhd,hde->jhe', key_part, state, precision=highest)
        grown = state + jnp.einsum('ihd,ihe->hde', query_part, grad_part)
        return (grown, (grad_query.astype(jnp.bfloat16), grad_key.astype(jnp.bfloat16), grad_value.astype(jnp.bfloat16)))
    final_grad, (grad_queries, grad_keys, grad_values) = lax.scan(backward_block, start_state, (query_blocks, key_blocks, value_blocks, grad_blocks, prefixes), reverse=True)
    width = heads * HEAD_DIM
    return (mixed, grad_queries.reshape(length, width), grad_keys.reshape(length, width), grad_values.reshape(length, width))
```

```python
import functools

import jax
import jax.numpy as jnp
from jax import lax
from jax.experimental import pallas as pl
from jax.experimental.pallas import tpu as pltpu
from jax.sharding import Mesh, PartitionSpec as P

HEAD_DIM = 128
HEADS_DEV = 4
TOK = 128
WIDTH = HEADS_DEV * HEAD_DIM
EPSILON = 1e-06
F32 = jnp.float32
BF16 = jnp.bfloat16
Z = ("z",)
CTX = ("y", "z")

NN = (((1,), (0,)), ((), ()))
NT = (((1,), (1,)), ((), ()))
TN = (((0,), (0,)), ((), ()))


def mm(a, b, dims):
    return lax.dot_general(a, b, dims, preferred_element_type=F32)


def head(h):
    return slice(h * HEAD_DIM, (h + 1) * HEAD_DIM)


def causal():
    rows = lax.broadcasted_iota(jnp.int32, (TOK, TOK), 0)
    cols = lax.broadcasted_iota(jnp.int32, (TOK, TOK), 1)
    return rows >= cols


def cost(flops, nbytes):
    return pl.CostEstimate(flops=flops, bytes_accessed=nbytes, transcendentals=0)


def state_kernel(k_ref, v_ref, out_ref):
    for h in range(HEADS_DEV):
        out_ref[head(h), :] = mm(k_ref[:, head(h)], v_ref[:, head(h)], TN).astype(out_ref.dtype)


def local_state(keys, values):
    return pl.pallas_call(
        state_kernel,
        out_shape=jax.ShapeDtypeStruct((WIDTH, HEAD_DIM), BF16),
        cost_estimate=cost(2 * TOK * WIDTH * HEAD_DIM, 400000),
        name="local_state",
    )(keys, values)


def scan_kernel(reverse, in_ref, out_ref):
    pairs = in_ref.shape[0] // 16
    total = jnp.zeros((8, HEAD_DIM), F32)
    order = range(pairs - 1, -1, -1) if reverse else range(pairs)
    for i in order:
        rows = slice(16 * i, 16 * i + 16)
        both = in_ref[rows, :].astype(F32)
        low, high = both[:8], both[8:]
        if reverse:
            then = total + high
            out_ref[rows, :] = jnp.concatenate([then, total], axis=0).astype(out_ref.dtype)
            total = then + low
        else:
            then = total + low
            out_ref[rows, :] = jnp.concatenate([total, then], axis=0).astype(out_ref.dtype)
            total = then + high


def exclusive_scan(pieces, reverse):
    return pl.pallas_call(
        functools.partial(scan_kernel, reverse),
        out_shape=jax.ShapeDtypeStruct(pieces.shape, pieces.dtype),
        cost_estimate=cost(WIDTH * HEAD_DIM, 300000),
        name="scan_states",
    )(pieces)


def carried(state, reverse):
    pieces = lax.all_to_all(state.reshape(64, 8, HEAD_DIM), CTX, 0, 0)
    sums = exclusive_scan(pieces.reshape(WIDTH, HEAD_DIM), reverse)
    back = lax.all_to_all(sums.reshape(64, 8, HEAD_DIM), CTX, 0, 0)
    return back.reshape(WIDTH, HEAD_DIM)


def attend_kernel(q_ref, k_ref, v_ref, s_ref, flat_ref, normed_ref, scale_ref, p_ref):
    keep = causal()
    for h in range(HEADS_DEV):
        q, k, v = q_ref[:, head(h)], k_ref[:, head(h)], v_ref[:, head(h)]
        weights = jnp.where(keep, mm(q, k, NT), 0.0).astype(BF16)
        p_ref[:, head(h)] = weights
        attended = mm(weights, v, NN) + mm(q, s_ref[head(h), :], NN)
        scale = lax.rsqrt(jnp.mean(attended * attended, axis=-1, keepdims=True) + EPSILON)
        normed = attended * scale
        flat_ref[:, head(h)] = normed.astype(BF16)
        normed_ref[:, head(h)] = normed
        scale_ref[:, head(h)] = jnp.broadcast_to(scale, (TOK, HEAD_DIM))


def attend(queries, keys, values, before):
    flat = jax.ShapeDtypeStruct((TOK, WIDTH), BF16)
    wide = jax.ShapeDtypeStruct((TOK, WIDTH), F32)
    return pl.pallas_call(
        attend_kernel,
        out_shape=(flat, wide, wide, flat),
        cost_estimate=cost(6 * TOK * WIDTH * HEAD_DIM, 1500000),
        name="attend",
    )(queries, keys, values, before)


def project_kernel(go_ref, w_ref, flat_ref, normed_ref, scale_ref, q_ref, part_ref, ga_ref, state_ref, gn_ref):
    step = pl.program_id(0)
    weight = w_ref[...]
    part_ref[0] = mm(flat_ref[...], weight, NT).astype(BF16)
    grad = mm(go_ref[0], weight, NN)

    @pl.when(step == 0)
    def _():
        gn_ref[...] = grad

    @pl.when(step > 0)
    def _():
        gn_ref[...] += grad

    @pl.when(step == pl.num_programs(0) - 1)
    def _():
        for h in range(HEADS_DEV):
            grad_normed, normed = gn_ref[:, head(h)], normed_ref[:, head(h)]
            mean = jnp.mean(grad_normed * normed, axis=-1, keepdims=True)
            ga = (scale_ref[:, head(h)] * (grad_normed - normed * mean)).astype(BF16)
            ga_ref[:, head(h)] = ga
            state_ref[head(h), :] = mm(q_ref[:, head(h)], ga, TN).astype(BF16)


def project(grad_full, weight, flat, normed, scale, queries):
    def group(j):
        return 2 * (j % 4) + j // 4

    whole = pl.BlockSpec((TOK, WIDTH), lambda j: (0, 0))
    return pl.pallas_call(
        project_kernel,
        grid=(8,),
        in_specs=[
            pl.BlockSpec((1, TOK, 512), lambda j: (j, 0, 0)),
            pl.BlockSpec((512, WIDTH), lambda j: (group(j), 0)),
            whole, whole, whole, whole,
        ],
        out_specs=(
            pl.BlockSpec((1, TOK, 512), lambda j: (group(j), 0, 0)),
            whole,
            pl.BlockSpec((WIDTH, HEAD_DIM), lambda j: (0, 0)),
        ),
        out_shape=(
            jax.ShapeDtypeStruct((8, TOK, 512), BF16),
            jax.ShapeDtypeStruct((TOK, WIDTH), BF16),
            jax.ShapeDtypeStruct((WIDTH, HEAD_DIM), BF16),
        ),
        scratch_shapes=[pltpu.VMEM((TOK, WIDTH), F32)],
        compiler_params=pltpu.CompilerParams(vmem_limit_bytes=24 * 1024 * 1024),
        cost_estimate=cost(4 * TOK * WIDTH * 4096, 8000000),
        name="project",
    )(grad_full, weight, flat, normed, scale, queries)


def grads_kernel(q_ref, k_ref, v_ref, p_ref, ga_ref, s_ref, g_ref, gq_ref, gk_ref, gv_ref):
    keep = causal()
    for h in range(HEADS_DEV):
        q, k, v, ga = q_ref[:, head(h)], k_ref[:, head(h)], v_ref[:, head(h)], ga_ref[:, head(h)]
        before, after = s_ref[head(h), :], g_ref[head(h), :]
        scores = jnp.where(keep, mm(ga, v, NT), 0.0).astype(BF16)
        gq_ref[:, head(h)] = (mm(scores, k, NN) + mm(ga, before, NT)).astype(BF16)
        gk_ref[:, head(h)] = (mm(scores, q, TN) + mm(v, after, NT)).astype(BF16)
        gv_ref[:, head(h)] = (mm(p_ref[:, head(h)], ga, TN) + mm(k, after, NN)).astype(BF16)


def grads(queries, keys, values, weights, ga, before, after):
    flat = jax.ShapeDtypeStruct((TOK, WIDTH), BF16)
    return pl.pallas_call(
        grads_kernel,
        out_shape=(flat, flat, flat),
        cost_estimate=cost(14 * TOK * WIDTH * HEAD_DIM, 1500000),
        name="grads",
    )(queries, keys, values, weights, ga, before, after)


def tied(first, second):
    return lax.optimization_barrier((first, second))


def local(queries, keys, values, out_weight, grad_out):
    mine = out_weight.T
    rows = lax.all_to_all(jnp.broadcast_to(mine, (8,) + mine.shape), Z, 0, 0)
    state = local_state(keys, values)
    rows, state = tied(rows, state)
    weight = lax.all_gather(rows.reshape(512, WIDTH), "y").reshape(4096, WIDTH)
    before = carried(state, False)
    flat, normed, scale, weights = attend(queries, keys, values, before)
    grad_out, flat = tied(grad_out, flat)
    along_x = lax.all_to_all(jnp.broadcast_to(grad_out, (4,) + grad_out.shape), "x", 0, 0)
    grad_full = lax.all_to_all(jnp.broadcast_to(along_x, (2,) + along_x.shape), "core", 0, 0)
    parts, ga, grad_state = project(
        grad_full.reshape(8, TOK, 512), weight, flat, normed, scale, queries
    )
    mixed = lax.psum_scatter(parts, ("x", "core"), scatter_dimension=0, tiled=False)
    after = carried(grad_state, True)
    grad_query, grad_key, grad_value = grads(queries, keys, values, weights, ga, before, after)
    return mixed, grad_query, grad_key, grad_value


def solution(mesh):
    finer = Mesh(mesh.devices.reshape(8, 8, 4, 2), ("y", "z", "x", "core"))
    spec = P(CTX, ("x", "core"))
    return jax.shard_map(
        local,
        mesh=finer,
        in_specs=(spec, spec, spec, P(("x", "core"), CTX), spec),
        out_specs=(spec, spec, spec, spec),
        check_vma=False,
    )
```

```python
import functools

import jax
import jax.numpy as jnp
from jax import lax
from jax.experimental import pallas as pl
from jax.experimental.pallas import tpu as pltpu
from jax.sharding import Mesh, PartitionSpec as P

HEAD_DIM = 128
HEADS_DEV = 4
TOK = 128
WIDTH = HEADS_DEV * HEAD_DIM
EPSILON = 1e-06
F32 = jnp.float32
BF16 = jnp.bfloat16
CTX = ("yh", "yl", "z")

NN = (((1,), (0,)), ((), ()))
NT = (((1,), (1,)), ((), ()))
TN = (((0,), (0,)), ((), ()))


def mm(a, b, dims):
    return lax.dot_general(a, b, dims, preferred_element_type=F32)


def head(h):
    return slice(h * HEAD_DIM, (h + 1) * HEAD_DIM)


def causal():
    rows = lax.broadcasted_iota(jnp.int32, (TOK, TOK), 0)
    cols = lax.broadcasted_iota(jnp.int32, (TOK, TOK), 1)
    return rows >= cols


def small():
    return pltpu.CompilerParams(vmem_limit_bytes=16 * 1024 * 1024)


def cost(flops, nbytes):
    return pl.CostEstimate(flops=flops, bytes_accessed=nbytes, transcendentals=0)


def state_kernel(k_ref, v_ref, out_ref):
    for h in range(HEADS_DEV):
        out_ref[head(h), :] = mm(k_ref[:, head(h)], v_ref[:, head(h)], TN).astype(out_ref.dtype)


def local_state(keys, values):
    return pl.pallas_call(
        state_kernel,
        out_shape=jax.ShapeDtypeStruct((WIDTH, HEAD_DIM), BF16),
        cost_estimate=cost(2 * TOK * WIDTH * HEAD_DIM, 400000),
        compiler_params=small(),
        name="local_state",
    )(keys, values)


def scan_kernel(reverse, in_ref, out_ref):
    pairs = in_ref.shape[0] // 16
    total = jnp.zeros((8, HEAD_DIM), F32)
    order = range(pairs - 1, -1, -1) if reverse else range(pairs)
    for i in order:
        rows = slice(16 * i, 16 * i + 16)
        both = in_ref[rows, :].astype(F32)
        low, high = both[:8], both[8:]
        if reverse:
            then = total + high
            out_ref[rows, :] = jnp.concatenate([then, total], axis=0).astype(out_ref.dtype)
            total = then + low
        else:
            then = total + low
            out_ref[rows, :] = jnp.concatenate([total, then], axis=0).astype(out_ref.dtype)
            total = then + high


def exclusive_scan(pieces, reverse):
    return pl.pallas_call(
        functools.partial(scan_kernel, reverse),
        out_shape=jax.ShapeDtypeStruct(pieces.shape, pieces.dtype),
        cost_estimate=cost(WIDTH * HEAD_DIM, 300000),
        compiler_params=small(),
        name="scan_states",
    )(pieces)


def carried(state, reverse):
    pieces = lax.all_to_all(state.reshape(64, 8, HEAD_DIM), CTX, 0, 0)
    sums = exclusive_scan(pieces.reshape(WIDTH, HEAD_DIM), reverse)
    back = lax.all_to_all(sums.reshape(64, 8, HEAD_DIM), CTX, 0, 0)
    return back.reshape(WIDTH, HEAD_DIM)


def attend_kernel(q_ref, k_ref, v_ref, s_ref, flat_ref, normed_ref, scale_ref, p_ref):
    keep = causal()
    for h in range(HEADS_DEV):
        q, k, v = q_ref[:, head(h)], k_ref[:, head(h)], v_ref[:, head(h)]
        weights = jnp.where(keep, mm(q, k, NT), 0.0).astype(BF16)
        p_ref[:, head(h)] = weights
        attended = mm(weights, v, NN) + mm(q, s_ref[head(h), :], NN)
        scale = lax.rsqrt(jnp.mean(attended * attended, axis=-1, keepdims=True) + EPSILON)
        normed = attended * scale
        flat_ref[:, head(h)] = normed.astype(BF16)
        normed_ref[:, head(h)] = normed
        scale_ref[:, head(h)] = jnp.broadcast_to(scale, (TOK, HEAD_DIM))


def attend(queries, keys, values, before):
    flat = jax.ShapeDtypeStruct((TOK, WIDTH), BF16)
    wide = jax.ShapeDtypeStruct((TOK, WIDTH), F32)
    return pl.pallas_call(
        attend_kernel,
        out_shape=(flat, wide, wide, flat),
        cost_estimate=cost(6 * TOK * WIDTH * HEAD_DIM, 1500000),
        compiler_params=small(),
        name="attend",
    )(queries, keys, values, before)


def project_kernel(place_ref, w_ref, go0_ref, go1_ref, go2_ref, go3_ref, mine_ref, other_ref, part_ref, own_ref, send_ref, w_buf, a_buf, out_buf, w_sem, out_sem):
    yl, x = place_ref[0], place_ref[1]
    own = pl.ds(pl.multiple_of(yl * TOK, TOK), TOK)
    other = pl.ds(pl.multiple_of((1 - yl) * TOK, TOK), TOK)
    groups = [lax.rem(x + r, 4) for r in range(4)]
    loads = [pltpu.make_async_copy(w_ref.at[:, groups[r]], w_buf.at[r], w_sem.at[r]) for r in range(4)]
    stores = [pltpu.make_async_copy(out_buf.at[r], part_ref.at[groups[r]], out_sem.at[r]) for r in range(4)]
    for load in loads:
        load.start()
    a_buf[own, :] = mine_ref[...]
    a_buf[other, :] = other_ref[...]
    normed = a_buf[...]
    grad = jnp.zeros((2 * TOK, WIDTH), F32)
    for r, go_ref in enumerate((go0_ref, go1_ref, go2_ref, go3_ref)):
        loads[r].wait()
        weight = w_buf[r].reshape(512, WIDTH)
        grad = grad + mm(go_ref[...].reshape(2 * TOK, 512), weight, NN)
        out_buf[r] = mm(normed, weight, NT).astype(BF16).reshape(2, TOK, 512)
        stores[r].start()
    first, second = grad[:TOK], grad[TOK:]
    own_ref[...] = jnp.where(yl == 0, first, second)
    send_ref[...] = jnp.where(yl == 0, second, first).astype(BF16)
    for store in stores:
        store.wait()


def project(weight, grad_parts, mine, other):
    vmem = pl.BlockSpec(memory_space=pltpu.VMEM)
    hbm = pl.BlockSpec(memory_space=pltpu.HBM)
    place = jnp.stack([lax.axis_index("yl"), lax.axis_index("x")]).astype(jnp.int32)
    return pl.pallas_call(
        project_kernel,
        in_specs=[pl.BlockSpec(memory_space=pltpu.SMEM), hbm] + [vmem] * 6,
        out_specs=(hbm, vmem, vmem),
        out_shape=(
            jax.ShapeDtypeStruct((4, 2, TOK, 512), BF16),
            jax.ShapeDtypeStruct((TOK, WIDTH), F32),
            jax.ShapeDtypeStruct((TOK, WIDTH), BF16),
        ),
        scratch_shapes=[
            pltpu.VMEM((4, 8, 64, WIDTH), BF16),
            pltpu.VMEM((2 * TOK, WIDTH), BF16),
            pltpu.VMEM((4, 2, TOK, 512), BF16),
            pltpu.SemaphoreType.DMA((4,)),
            pltpu.SemaphoreType.DMA((4,)),
        ],
        compiler_params=small(),
        cost_estimate=cost(4 * TOK * WIDTH * 4096, 6000000),
        name="project",
    )(place, weight, *grad_parts, mine, other)


def grad_attended_kernel(own_ref, got_ref, normed_ref, scale_ref, q_ref, ga_ref, state_ref):
    for h in range(HEADS_DEV):
        grad_normed = own_ref[:, head(h)] + got_ref[:, head(h)].astype(F32)
        normed = normed_ref[:, head(h)]
        mean = jnp.mean(grad_normed * normed, axis=-1, keepdims=True)
        ga = (scale_ref[:, head(h)] * (grad_normed - normed * mean)).astype(BF16)
        ga_ref[:, head(h)] = ga
        state_ref[head(h), :] = mm(q_ref[:, head(h)], ga, TN).astype(BF16)


def grad_attended(own, got, normed, scale, queries):
    return pl.pallas_call(
        grad_attended_kernel,
        out_shape=(
            jax.ShapeDtypeStruct((TOK, WIDTH), BF16),
            jax.ShapeDtypeStruct((WIDTH, HEAD_DIM), BF16),
        ),
        compiler_params=small(),
        cost_estimate=cost(2 * TOK * WIDTH * HEAD_DIM, 1200000),
        name="grad_attended",
    )(own, got, normed, scale, queries)


def grads_kernel(q_ref, k_ref, v_ref, p_ref, ga_ref, s_ref, g_ref, gq_ref, gk_ref, gv_ref):
    keep = causal()
    for h in range(HEADS_DEV):
        q, k, v, ga = q_ref[:, head(h)], k_ref[:, head(h)], v_ref[:, head(h)], ga_ref[:, head(h)]
        before, after = s_ref[head(h), :], g_ref[head(h), :]
        scores = jnp.where(keep, mm(ga, v, NT), 0.0).astype(BF16)
        gq_ref[:, head(h)] = (mm(scores, k, NN) + mm(ga, before, NT)).astype(BF16)
        gk_ref[:, head(h)] = (mm(scores, q, TN) + mm(v, after, NT)).astype(BF16)
        gv_ref[:, head(h)] = (mm(p_ref[:, head(h)], ga, TN) + mm(k, after, NN)).astype(BF16)


def grads(queries, keys, values, weights, ga, before, after):
    flat = jax.ShapeDtypeStruct((TOK, WIDTH), BF16)
    return pl.pallas_call(
        grads_kernel,
        out_shape=(flat, flat, flat),
        cost_estimate=cost(14 * TOK * WIDTH * HEAD_DIM, 1500000),
        compiler_params=small(),
        name="grads",
    )(queries, keys, values, weights, ga, before, after)


def tied(first, second):
    return lax.optimization_barrier((first, second))


SWAP = [(0, 1), (1, 0)]
TRANSPOSE = [(0, 0), (1, 2), (2, 1), (3, 3)]


def repeated(value, times):
    return jnp.broadcast_to(value, (times,) + value.shape)


def shifted(value, step):
    return lax.ppermute(value, "x", [((i + step) % 4, i) for i in range(4)])


def local(queries, keys, values, out_weight, grad_out):
    grad_turned = lax.ppermute(grad_out, ("yl", "core"), TRANSPOSE)
    rows = lax.all_to_all(repeated(out_weight.T, 4), "yh", 0, 0)
    state = local_state(keys, values)
    rows, state = tied(rows, state)
    weight = lax.all_gather(rows, "z")
    grad_other = lax.ppermute(grad_turned, "core", SWAP)
    core = lax.axis_index("core")
    grad_own = jnp.stack(
        [jnp.where(core == 0, grad_turned, grad_other), jnp.where(core == 0, grad_other, grad_turned)]
    )
    before = carried(state, False)
    flat, normed, scale, weights = attend(queries, keys, values, before)
    flat_other = lax.ppermute(flat, "yl", SWAP)
    grad_parts = [grad_own] + [shifted(grad_own, r) for r in (1, 2, 3)]
    parts, own, send = project(weight, grad_parts, flat, flat_other)
    got = lax.ppermute(send, "yl", SWAP)
    mixed_turned = lax.psum_scatter(
        parts.reshape(8, TOK, 512), ("x", "core"), scatter_dimension=0, tiled=False
    )
    ga, grad_state = grad_attended(own, got, normed, scale, queries)
    after = carried(grad_state, True)
    grad_query, grad_key, grad_value = grads(queries, keys, values, weights, ga, before, after)
    mixed = lax.ppermute(mixed_turned, ("yl", "core"), TRANSPOSE)
    return mixed, grad_query, grad_key, grad_value


def solution(mesh):
    finer = Mesh(mesh.devices.reshape(4, 2, 8, 4, 2), ("yh", "yl", "z", "x", "core"))
    spec = P(CTX, ("x", "core"))
    return jax.shard_map(
        local,
        mesh=finer,
        in_specs=(spec, spec, spec, P(("x", "core"), CTX), spec),
        out_specs=(spec, spec, spec, spec),
        check_vma=False,
    )
```

```python
import functools

import jax
import jax.numpy as jnp
from jax import lax
from jax.experimental import pallas as pl
from jax.experimental.pallas import tpu as pltpu
from jax.sharding import Mesh, PartitionSpec as P

HEAD_DIM = 128
HEADS_DEV = 4
TOK = 128
WIDTH = HEADS_DEV * HEAD_DIM
EPSILON = 1e-06
F32 = jnp.float32
BF16 = jnp.bfloat16
CTX = ("y", "zh", "zl")

NN = (((1,), (0,)), ((), ()))
NT = (((1,), (1,)), ((), ()))
TN = (((0,), (0,)), ((), ()))


def mm(a, b, dims):
    return lax.dot_general(a, b, dims, preferred_element_type=F32)


def head(h):
    return slice(h * HEAD_DIM, (h + 1) * HEAD_DIM)


def causal():
    rows = lax.broadcasted_iota(jnp.int32, (TOK, TOK), 0)
    cols = lax.broadcasted_iota(jnp.int32, (TOK, TOK), 1)
    return rows >= cols


def small():
    return pltpu.CompilerParams(vmem_limit_bytes=16 * 1024 * 1024)


def cost(flops, nbytes):
    return pl.CostEstimate(flops=flops, bytes_accessed=nbytes, transcendentals=0)


def blocks_of(value, parity):
    return jnp.concatenate(
        [value[:, 128 * j + 64 * parity : 128 * j + 64 * parity + 64] for j in range(4)], axis=1
    )


def vmem():
    return pl.BlockSpec(memory_space=pltpu.VMEM)


def hbm():
    return pl.BlockSpec(memory_space=pltpu.HBM)


def smem():
    return pl.BlockSpec(memory_space=pltpu.SMEM)


def in_hbm(value):
    return pltpu.with_memory_space_constraint(value, pltpu.HBM)


def state_kernel(k_ref, v_ref, out_ref):
    for h in range(HEADS_DEV):
        out_ref[head(h), :] = mm(k_ref[:, head(h)], v_ref[:, head(h)], TN).astype(BF16)


def local_state(keys, values):
    return pl.pallas_call(
        state_kernel,
        out_shape=jax.ShapeDtypeStruct((WIDTH, HEAD_DIM), BF16),
        compiler_params=small(),
        cost_estimate=cost(2 * TOK * WIDTH * HEAD_DIM, 400000),
        name="local_state",
    )(keys, values)


def split_kernel(place_ref, go_ref, keep_ref, send_ref):
    value = go_ref[...].astype(F32)
    even, odd = blocks_of(value, 0).astype(BF16), blocks_of(value, 1).astype(BF16)
    first = place_ref[0] == 0
    keep_ref[...] = jnp.where(first, even, odd)
    send_ref[...] = jnp.where(first, odd, even)


def split_columns(place, grad_out):
    half = jax.ShapeDtypeStruct((TOK, 256), BF16)
    return pl.pallas_call(
        split_kernel,
        in_specs=[smem(), vmem()],
        out_shape=(half, half),
        compiler_params=small(),
        cost_estimate=cost(TOK * WIDTH, 300000),
        name="split_columns",
    )(place, grad_out)


def scan_kernel(reverse, in_ref, out_ref):
    pairs = in_ref.shape[0] // 16
    total = jnp.zeros((8, HEAD_DIM), F32)
    order = range(pairs - 1, -1, -1) if reverse else range(pairs)
    for i in order:
        rows = slice(16 * i, 16 * i + 16)
        both = in_ref[rows, :].astype(F32)
        low, high = both[:8], both[8:]
        if reverse:
            then = total + high
            out_ref[rows, :] = jnp.concatenate([then, total], axis=0).astype(out_ref.dtype)
            total = then + low
        else:
            then = total + low
            out_ref[rows, :] = jnp.concatenate([total, then], axis=0).astype(out_ref.dtype)
            total = then + high


def exclusive_scan(pieces, reverse):
    return pl.pallas_call(
        functools.partial(scan_kernel, reverse),
        out_shape=jax.ShapeDtypeStruct(pieces.shape, pieces.dtype),
        cost_estimate=cost(WIDTH * HEAD_DIM, 300000),
        compiler_params=small(),
        name="scan_states",
    )(pieces)


def carried(state, reverse):
    pieces = lax.all_to_all(state.reshape(64, 8, HEAD_DIM), CTX, 0, 0)
    sums = exclusive_scan(pieces.reshape(WIDTH, HEAD_DIM), reverse)
    back = lax.all_to_all(sums.reshape(64, 8, HEAD_DIM), CTX, 0, 0)
    return back.reshape(WIDTH, HEAD_DIM)


def attend_kernel(q_ref, k_ref, v_ref, s_ref, flat_ref, normed_ref, scale_ref, p_ref):
    keep = causal()
    for h in range(HEADS_DEV):
        q, k, v = q_ref[:, head(h)], k_ref[:, head(h)], v_ref[:, head(h)]
        weights = jnp.where(keep, mm(q, k, NT), 0.0).astype(BF16)
        p_ref[:, head(h)] = weights
        attended = mm(weights, v, NN) + mm(q, s_ref[head(h), :], NN)
        scale = lax.rsqrt(jnp.mean(attended * attended, axis=-1, keepdims=True) + EPSILON)
        normed = attended * scale
        flat_ref[:, head(h)] = normed.astype(BF16)
        normed_ref[:, head(h)] = normed
        scale_ref[:, head(h)] = jnp.broadcast_to(scale, (TOK, HEAD_DIM))


def attend(queries, keys, values, before):
    flat = jax.ShapeDtypeStruct((TOK, WIDTH), BF16)
    wide = jax.ShapeDtypeStruct((TOK, WIDTH), F32)
    return pl.pallas_call(
        attend_kernel,
        out_shape=(flat, wide, wide, flat),
        cost_estimate=cost(6 * TOK * WIDTH * HEAD_DIM, 1500000),
        compiler_params=small(),
        name="attend",
    )(queries, keys, values, before)


def grad_normed_kernel(place_ref, w_ref, go0_ref, go1_ref, go3_ref, go2_ref, far_ref, own_ref, send_ref, w_buf, w_sem):
    x, core = place_ref[1], place_ref[2]
    groups = [2 * lax.rem(x + r, 4) + cs for r in (0, 1, 3, 2) for cs in (core, 1 - core)]
    pieces = [ref.at[i] for ref in (go0_ref, go1_ref, go3_ref) for i in range(2)] + [go2_ref, far_ref]
    loads = [pltpu.make_async_copy(w_ref.at[g], w_buf.at[g], w_sem.at[i]) for i, g in enumerate(groups)]
    for load in loads:
        load.start()
    grad = jnp.zeros((2 * TOK, WIDTH), F32)
    for i in range(8):
        loads[i].wait()
        grad = grad + mm(pieces[i][...].reshape(2 * TOK, 256), w_buf[groups[i]], NN)
    own_ref[...] = grad[:TOK]
    send_ref[...] = grad[TOK:].astype(BF16)


def grad_normed_parts(place, weight, grad_parts):
    return pl.pallas_call(
        grad_normed_kernel,
        in_specs=[smem(), hbm()] + [vmem()] * 5,
        out_specs=(vmem(), vmem(), vmem()),
        out_shape=(
            jax.ShapeDtypeStruct((TOK, WIDTH), F32),
            jax.ShapeDtypeStruct((TOK, WIDTH), BF16),
            jax.ShapeDtypeStruct((8, 256, WIDTH), BF16),
        ),
        scratch_shapes=[pltpu.SemaphoreType.DMA((8,))],
        compiler_params=small(),
        cost_estimate=cost(2 * TOK * WIDTH * 4096, 4000000),
        name="grad_normed",
    )(place, weight, *grad_parts)


def project_kernel(w_ref, own_ref, other_ref, part_ref, out_buf, out_sem):
    stores = [pltpu.make_async_copy(out_buf.at[g], part_ref.at[g], out_sem.at[g]) for g in range(8)]
    normed = jnp.concatenate([own_ref[...], other_ref[...]], axis=0)
    for g in range(8):
        out_buf[g] = mm(normed, w_ref[g], NT).astype(BF16).reshape(2, TOK, 256)
        stores[g].start()
    for store in stores:
        store.wait()


def project(weight, own, other):
    return pl.pallas_call(
        project_kernel,
        in_specs=[vmem()] * 3,
        out_specs=hbm(),
        out_shape=jax.ShapeDtypeStruct((8, 2, TOK, 256), BF16),
        scratch_shapes=[pltpu.VMEM((8, 2, TOK, 256), BF16), pltpu.SemaphoreType.DMA((8,))],
        compiler_params=small(),
        cost_estimate=cost(2 * TOK * WIDTH * 4096, 4000000),
        name="project",
    )(weight, own, other)


def grad_attended_kernel(own_ref, got_ref, normed_ref, scale_ref, q_ref, ga_ref, state_ref):
    for h in range(HEADS_DEV):
        grad_normed = own_ref[:, head(h)] + got_ref[:, head(h)].astype(F32)
        normed = normed_ref[:, head(h)]
        mean = jnp.mean(grad_normed * normed, axis=-1, keepdims=True)
        ga = (scale_ref[:, head(h)] * (grad_normed - normed * mean)).astype(BF16)
        ga_ref[:, head(h)] = ga
        state_ref[head(h), :] = mm(q_ref[:, head(h)], ga, TN).astype(BF16)


def grad_attended(own, got, normed, scale, queries):
    return pl.pallas_call(
        grad_attended_kernel,
        out_shape=(
            jax.ShapeDtypeStruct((TOK, WIDTH), BF16),
            jax.ShapeDtypeStruct((WIDTH, HEAD_DIM), BF16),
        ),
        compiler_params=small(),
        cost_estimate=cost(2 * TOK * WIDTH * HEAD_DIM, 1200000),
        name="grad_attended",
    )(own, got, normed, scale, queries)


def grads_block_kernel(q_ref, k_ref, v_ref, p_ref, ga_ref, s_ref, gq_ref, gk_ref, gv_ref):
    keep = causal()
    for h in range(HEADS_DEV):
        q, k, v, ga = q_ref[:, head(h)], k_ref[:, head(h)], v_ref[:, head(h)], ga_ref[:, head(h)]
        scores = jnp.where(keep, mm(ga, v, NT), 0.0).astype(BF16)
        gq_ref[:, head(h)] = (mm(scores, k, NN) + mm(ga, s_ref[head(h), :], NT)).astype(BF16)
        gk_ref[:, head(h)] = mm(scores, q, TN)
        gv_ref[:, head(h)] = mm(p_ref[:, head(h)], ga, TN)


def grads_block(queries, keys, values, weights, ga, before):
    flat = jax.ShapeDtypeStruct((TOK, WIDTH), BF16)
    wide = jax.ShapeDtypeStruct((TOK, WIDTH), F32)
    return pl.pallas_call(
        grads_block_kernel,
        out_shape=(flat, wide, wide),
        compiler_params=small(),
        cost_estimate=cost(10 * TOK * WIDTH * HEAD_DIM, 1500000),
        name="grads_block",
    )(queries, keys, values, weights, ga, before)


def finish_kernel(place_ref, k_ref, v_ref, g_ref, gk_in_ref, gv_in_ref, keep_ref, got_ref, mixed_ref, gk_ref, gv_ref):
    keep, got = keep_ref[...].astype(F32), got_ref[...].astype(F32)
    first = place_ref[0] == 0
    even, odd = jnp.where(first, keep, got), jnp.where(first, got, keep)
    for j in range(4):
        cols = slice(64 * j, 64 * j + 64)
        mixed_ref[:, head(j)] = jnp.concatenate([even[:, cols], odd[:, cols]], axis=1).astype(BF16)
    for h in range(HEADS_DEV):
        after = g_ref[head(h), :]
        gk_ref[:, head(h)] = (gk_in_ref[:, head(h)] + mm(v_ref[:, head(h)], after, NT)).astype(BF16)
        gv_ref[:, head(h)] = (gv_in_ref[:, head(h)] + mm(k_ref[:, head(h)], after, NN)).astype(BF16)


def finish(place, keys, values, after, grad_key, grad_value, keep, got):
    flat = jax.ShapeDtypeStruct((TOK, WIDTH), BF16)
    return pl.pallas_call(
        finish_kernel,
        in_specs=[smem()] + [vmem()] * 7,
        out_shape=(flat, flat, flat),
        compiler_params=small(),
        cost_estimate=cost(4 * TOK * WIDTH * HEAD_DIM, 1500000),
        name="finish",
    )(place, keys, values, after, grad_key, grad_value, keep, got)


def tied(first, second):
    return lax.optimization_barrier((first, second))


SWAP = [(0, 1), (1, 0)]


def repeated(value, times):
    return jnp.broadcast_to(value, (times,) + value.shape)


def shifted(value, axis, step):
    return lax.ppermute(value, axis, [((i + step) % 4, i) for i in range(4)])


def local(queries, keys, values, out_weight, grad_out):
    place = jnp.stack([lax.axis_index(n) for n in ("zl", "x", "core")]).astype(jnp.int32)
    rows = lax.all_to_all(repeated(out_weight.T, 4), "zh", 0, 0)
    grad_keep, grad_send = split_columns(place, in_hbm(grad_out))
    grad_got = lax.ppermute(grad_send, "zl", SWAP)
    state = local_state(in_hbm(keys), in_hbm(values))
    (grad_got, rows), state = tied((grad_got, rows), state)
    grad_pair = jnp.stack([grad_keep, grad_got])
    weight = lax.all_gather(rows, "y").reshape(8, 256, WIDTH)
    weight = in_hbm(weight)
    grad_cores = jnp.stack([grad_pair, lax.ppermute(grad_pair, "core", SWAP)])
    grad_far = shifted(grad_pair, "x", 2)
    grad_parts = [grad_cores] + [shifted(grad_cores, "x", r) for r in (1, 3)]
    grad_parts += [grad_far, lax.ppermute(grad_far, "core", SWAP)]
    before = carried(state, False)
    flat, normed, scale, weights = attend(queries, keys, values, before)
    flat_other = lax.ppermute(flat, "zl", SWAP)
    own, send, weight = grad_normed_parts(place, weight, grad_parts)
    flat, send = tied(flat, send)
    got = lax.ppermute(send, "zl", SWAP)
    parts = project(weight, flat, flat_other)
    mixed_pair = lax.psum_scatter(parts, ("x", "core"), scatter_dimension=0, tiled=False)
    ga, grad_state = grad_attended(own, got, normed, scale, queries)
    after = carried(grad_state, True)
    grad_query, grad_key, grad_value = grads_block(queries, keys, values, weights, ga, before)
    mixed_got = lax.ppermute(mixed_pair[1], "zl", SWAP)
    mixed, grad_key, grad_value = finish(
        place, keys, values, after, grad_key, grad_value, mixed_pair[0], mixed_got
    )
    return mixed, grad_query, grad_key, grad_value


def solution(mesh):
    finer = Mesh(mesh.devices.reshape(8, 4, 2, 4, 2), ("y", "zh", "zl", "x", "core"))
    spec = P(CTX, ("x", "core"))
    return jax.shard_map(
        local,
        mesh=finer,
        in_specs=(spec, spec, spec, P(("x", "core"), CTX), spec),
        out_specs=(spec, spec, spec, spec),
        check_vma=False,
    )
```

```python
import functools

import jax
import jax.numpy as jnp
from jax import lax
from jax.experimental import pallas as pl
from jax.experimental.pallas import tpu as pltpu
from jax.sharding import Mesh, PartitionSpec as P

HEAD_DIM = 128
HEADS_DEV = 4
TOK = 128
WIDTH = HEADS_DEV * HEAD_DIM
EPSILON = 1e-06
F32 = jnp.float32
BF16 = jnp.bfloat16
CTX = ("y", "zh", "zl")

NN = (((1,), (0,)), ((), ()))
NT = (((1,), (1,)), ((), ()))
TN = (((0,), (0,)), ((), ()))


def mm(a, b, dims):
    return lax.dot_general(a, b, dims, preferred_element_type=F32)


def head(h):
    return slice(h * HEAD_DIM, (h + 1) * HEAD_DIM)


def causal():
    rows = lax.broadcasted_iota(jnp.int32, (TOK, TOK), 0)
    cols = lax.broadcasted_iota(jnp.int32, (TOK, TOK), 1)
    return rows >= cols


def small():
    return pltpu.CompilerParams(vmem_limit_bytes=16 * 1024 * 1024)


def cost(flops, nbytes):
    return pl.CostEstimate(flops=flops, bytes_accessed=nbytes, transcendentals=0)


def blocks_of(value, parity):
    return jnp.concatenate(
        [value[:, 128 * j + 64 * parity : 128 * j + 64 * parity + 64] for j in range(4)], axis=1
    )


def vmem():
    return pl.BlockSpec(memory_space=pltpu.VMEM)


def hbm():
    return pl.BlockSpec(memory_space=pltpu.HBM)


def smem():
    return pl.BlockSpec(memory_space=pltpu.SMEM)


def in_hbm(value):
    return pltpu.with_memory_space_constraint(value, pltpu.HBM)


def state_kernel(k_ref, v_ref, out_ref):
    for h in range(HEADS_DEV):
        out_ref[head(h), :] = mm(k_ref[:, head(h)], v_ref[:, head(h)], TN).astype(BF16)


def local_state(keys, values):
    return pl.pallas_call(
        state_kernel,
        out_shape=jax.ShapeDtypeStruct((WIDTH, HEAD_DIM), BF16),
        compiler_params=small(),
        cost_estimate=cost(2 * TOK * WIDTH * HEAD_DIM, 400000),
        name="local_state",
    )(keys, values)


def split_kernel(place_ref, go_ref, keep_ref, send_ref):
    value = go_ref[...].astype(F32)
    even, odd = blocks_of(value, 0).astype(BF16), blocks_of(value, 1).astype(BF16)
    first = place_ref[0] == 0
    keep_ref[...] = jnp.where(first, even, odd)
    send_ref[...] = jnp.where(first, odd, even)


def split_columns(place, grad_out):
    half = jax.ShapeDtypeStruct((TOK, 256), BF16)
    return pl.pallas_call(
        split_kernel,
        in_specs=[smem(), vmem()],
        out_shape=(half, half),
        compiler_params=small(),
        cost_estimate=cost(TOK * WIDTH, 300000),
        name="split_columns",
    )(place, grad_out)


def scan_kernel(reverse, in_ref, out_ref):
    pairs = in_ref.shape[0] // 16
    total = jnp.zeros((8, HEAD_DIM), F32)
    order = range(pairs - 1, -1, -1) if reverse else range(pairs)
    for i in order:
        rows = slice(16 * i, 16 * i + 16)
        both = in_ref[rows, :].astype(F32)
        low, high = both[:8], both[8:]
        if reverse:
            then = total + high
            out_ref[rows, :] = jnp.concatenate([then, total], axis=0).astype(out_ref.dtype)
            total = then + low
        else:
            then = total + low
            out_ref[rows, :] = jnp.concatenate([total, then], axis=0).astype(out_ref.dtype)
            total = then + high


def exclusive_scan(pieces, reverse):
    return pl.pallas_call(
        functools.partial(scan_kernel, reverse),
        out_shape=jax.ShapeDtypeStruct(pieces.shape, pieces.dtype),
        cost_estimate=cost(WIDTH * HEAD_DIM, 300000),
        compiler_params=small(),
        name="scan_states",
    )(pieces)


def carried(state, reverse):
    pieces = lax.all_to_all(state.reshape(64, 8, HEAD_DIM), CTX, 0, 0)
    sums = exclusive_scan(pieces.reshape(WIDTH, HEAD_DIM), reverse)
    back = lax.all_to_all(sums.reshape(64, 8, HEAD_DIM), CTX, 0, 0)
    return back.reshape(WIDTH, HEAD_DIM)


def attend_kernel(q_ref, k_ref, v_ref, s_ref, flat_ref, normed_ref, scale_ref, p_ref):
    keep = causal()
    for h in range(HEADS_DEV):
        q, k, v = q_ref[:, head(h)], k_ref[:, head(h)], v_ref[:, head(h)]
        weights = jnp.where(keep, mm(q, k, NT), 0.0).astype(BF16)
        p_ref[:, head(h)] = weights
        attended = mm(weights, v, NN) + mm(q, s_ref[head(h), :], NN)
        scale = lax.rsqrt(jnp.mean(attended * attended, axis=-1, keepdims=True) + EPSILON)
        normed = attended * scale
        flat_ref[:, head(h)] = normed.astype(BF16)
        normed_ref[:, head(h)] = normed
        scale_ref[:, head(h)] = jnp.broadcast_to(scale, (TOK, HEAD_DIM))


def attend(queries, keys, values, before):
    flat = jax.ShapeDtypeStruct((TOK, WIDTH), BF16)
    wide = jax.ShapeDtypeStruct((TOK, WIDTH), F32)
    return pl.pallas_call(
        attend_kernel,
        out_shape=(flat, wide, wide, flat),
        cost_estimate=cost(6 * TOK * WIDTH * HEAD_DIM, 1500000),
        compiler_params=small(),
        name="attend",
    )(queries, keys, values, before)


def grad_normed_kernel(place_ref, w_ref, go0_ref, go1_ref, go3_ref, go2_ref, far_ref, own_ref, send_ref, w_buf, w_sem):
    x, core = place_ref[1], place_ref[2]
    groups = [2 * lax.rem(x + r, 4) + cs for r in (0, 1, 3, 2) for cs in (core, 1 - core)]
    pieces = [ref.at[i] for ref in (go0_ref, go1_ref, go3_ref) for i in range(2)] + [go2_ref, far_ref]
    loads = [pltpu.make_async_copy(w_ref.at[g], w_buf.at[g], w_sem.at[i]) for i, g in enumerate(groups)]
    for load in loads:
        load.start()
    grad = jnp.zeros((2 * TOK, WIDTH), F32)
    for i in range(8):
        loads[i].wait()
        grad = grad + mm(pieces[i][...].reshape(2 * TOK, 256), w_buf[groups[i]], NN)
    own_ref[...] = grad[:TOK]
    send_ref[...] = grad[TOK:]


def grad_normed_parts(place, weight, grad_parts):
    return pl.pallas_call(
        grad_normed_kernel,
        in_specs=[smem(), hbm()] + [vmem()] * 5,
        out_specs=(vmem(), vmem(), vmem()),
        out_shape=(
            jax.ShapeDtypeStruct((TOK, WIDTH), F32),
            jax.ShapeDtypeStruct((TOK, WIDTH), F32),
            jax.ShapeDtypeStruct((8, 256, WIDTH), BF16),
        ),
        scratch_shapes=[pltpu.SemaphoreType.DMA((8,))],
        compiler_params=small(),
        cost_estimate=cost(2 * TOK * WIDTH * 4096, 4000000),
        name="grad_normed",
    )(place, weight, *grad_parts)


def project_kernel(w_ref, own_ref, other_ref, part_ref, out_buf, out_sem):
    stores = [pltpu.make_async_copy(out_buf.at[g], part_ref.at[g], out_sem.at[g]) for g in range(8)]
    normed = jnp.concatenate([own_ref[...], other_ref[...]], axis=0)
    for g in range(8):
        out_buf[g] = mm(normed, w_ref[g], NT).astype(BF16).reshape(2, TOK, 256)
        stores[g].start()
    for store in stores:
        store.wait()


def project(weight, own, other):
    return pl.pallas_call(
        project_kernel,
        in_specs=[vmem()] * 3,
        out_specs=hbm(),
        out_shape=jax.ShapeDtypeStruct((8, 2, TOK, 256), BF16),
        scratch_shapes=[pltpu.VMEM((8, 2, TOK, 256), BF16), pltpu.SemaphoreType.DMA((8,))],
        compiler_params=small(),
        cost_estimate=cost(10000000000, 40000000),
        name="project",
    )(weight, own, other)


def grad_attended_kernel(own_ref, got_ref, normed_ref, scale_ref, q_ref, ga_ref, state_ref):
    for h in range(HEADS_DEV):
        grad_normed = own_ref[:, head(h)] + got_ref[:, head(h)]
        normed = normed_ref[:, head(h)]
        mean = jnp.mean(grad_normed * normed, axis=-1, keepdims=True)
        ga = (scale_ref[:, head(h)] * (grad_normed - normed * mean)).astype(BF16)
        ga_ref[:, head(h)] = ga
        state_ref[head(h), :] = mm(q_ref[:, head(h)], ga, TN).astype(BF16)


def grad_attended(own, got, normed, scale, queries):
    return pl.pallas_call(
        grad_attended_kernel,
        out_shape=(
            jax.ShapeDtypeStruct((TOK, WIDTH), BF16),
            jax.ShapeDtypeStruct((WIDTH, HEAD_DIM), BF16),
        ),
        compiler_params=small(),
        cost_estimate=cost(30000000000, 100000000),
        name="grad_attended",
    )(own, got, normed, scale, queries)


def grads_block_kernel(q_ref, k_ref, v_ref, p_ref, ga_ref, s_ref, gq_ref, gk_ref, gv_ref):
    keep = causal()
    for h in range(HEADS_DEV):
        q, k, v, ga = q_ref[:, head(h)], k_ref[:, head(h)], v_ref[:, head(h)], ga_ref[:, head(h)]
        scores = jnp.where(keep, mm(ga, v, NT), 0.0).astype(BF16)
        gq_ref[:, head(h)] = (mm(scores, k, NN) + mm(ga, s_ref[head(h), :], NT)).astype(BF16)
        gk_ref[:, head(h)] = mm(scores, q, TN)
        gv_ref[:, head(h)] = mm(p_ref[:, head(h)], ga, TN)


def grads_block(queries, keys, values, weights, ga, before):
    flat = jax.ShapeDtypeStruct((TOK, WIDTH), BF16)
    wide = jax.ShapeDtypeStruct((TOK, WIDTH), F32)
    return pl.pallas_call(
        grads_block_kernel,
        out_shape=(flat, wide, wide),
        compiler_params=small(),
        cost_estimate=cost(10 * TOK * WIDTH * HEAD_DIM, 1500000),
        name="grads_block",
    )(queries, keys, values, weights, ga, before)


def finish_kernel(place_ref, k_ref, v_ref, g_ref, gk_in_ref, gv_in_ref, keep_ref, got_ref, mixed_ref, gk_ref, gv_ref):
    keep, got = keep_ref[...].astype(F32), got_ref[...].astype(F32)
    first = place_ref[0] == 0
    even, odd = jnp.where(first, keep, got), jnp.where(first, got, keep)
    for j in range(4):
        cols = slice(64 * j, 64 * j + 64)
        mixed_ref[:, head(j)] = jnp.concatenate([even[:, cols], odd[:, cols]], axis=1).astype(BF16)
    for h in range(HEADS_DEV):
        after = g_ref[head(h), :]
        gk_ref[:, head(h)] = (gk_in_ref[:, head(h)] + mm(v_ref[:, head(h)], after, NT)).astype(BF16)
        gv_ref[:, head(h)] = (gv_in_ref[:, head(h)] + mm(k_ref[:, head(h)], after, NN)).astype(BF16)


def finish(place, keys, values, after, grad_key, grad_value, keep, got):
    flat = jax.ShapeDtypeStruct((TOK, WIDTH), BF16)
    return pl.pallas_call(
        finish_kernel,
        in_specs=[smem()] + [vmem()] * 7,
        out_shape=(flat, flat, flat),
        compiler_params=small(),
        cost_estimate=cost(4 * TOK * WIDTH * HEAD_DIM, 1500000),
        name="finish",
    )(place, keys, values, after, grad_key, grad_value, keep, got)


def tied(first, second):
    return lax.optimization_barrier((first, second))


SWAP = [(0, 1), (1, 0)]


def repeated(value, times):
    return jnp.broadcast_to(value, (times,) + value.shape)


def shifted(value, axis, step):
    return lax.ppermute(value, axis, [((i + step) % 4, i) for i in range(4)])


def local(queries, keys, values, out_weight, grad_out):
    place = jnp.stack([lax.axis_index(n) for n in ("zl", "x", "core")]).astype(jnp.int32)
    rows = lax.all_to_all(repeated(out_weight.T, 4), "zh", 0, 0)
    grad_keep, grad_send = split_columns(place, in_hbm(grad_out))
    grad_got = lax.ppermute(grad_send, "zl", SWAP)
    state = local_state(in_hbm(keys), in_hbm(values))
    (grad_got, rows), state = tied((grad_got, rows), state)
    grad_pair = jnp.stack([grad_keep, grad_got])
    weight = lax.all_gather(rows, "y").reshape(8, 256, WIDTH)
    weight = in_hbm(weight)
    grad_cores = jnp.stack([grad_pair, lax.ppermute(grad_pair, "core", SWAP)])
    grad_far = shifted(grad_pair, "x", 2)
    grad_parts = [grad_cores] + [shifted(grad_cores, "x", r) for r in (1, 3)]
    grad_parts += [grad_far, lax.ppermute(grad_far, "core", SWAP)]
    before = carried(state, False)
    flat, normed, scale, weights = attend(queries, keys, values, before)
    flat_other = lax.ppermute(flat, "zl", SWAP)
    own, send, weight = grad_normed_parts(place, weight, grad_parts)
    flat, send = tied(flat, send)
    got = lax.ppermute(send, "zl", SWAP)
    parts = project(weight, flat, flat_other)
    mixed_pair = lax.psum_scatter(parts, ("x", "core"), scatter_dimension=0, tiled=False)
    ga, grad_state = grad_attended(own, got, normed, scale, queries)
    after = carried(grad_state, True)
    grad_query, grad_key, grad_value = grads_block(queries, keys, values, weights, ga, before)
    mixed_got = lax.ppermute(mixed_pair[1], "zl", SWAP)
    mixed, grad_key, grad_value = finish(
        place, keys, values, after, grad_key, grad_value, mixed_pair[0], mixed_got
    )
    return mixed, grad_query, grad_key, grad_value


def solution(mesh):
    finer = Mesh(mesh.devices.reshape(8, 4, 2, 4, 2), ("y", "zh", "zl", "x", "core"))
    spec = P(CTX, ("x", "core"))
    return jax.shard_map(
        local,
        mesh=finer,
        in_specs=(spec, spec, spec, P(("x", "core"), CTX), spec),
        out_specs=(spec, spec, spec, spec),
        check_vma=False,
    )
```

```python
import functools

import jax
import jax.numpy as jnp
from jax import lax
from jax.experimental import pallas as pl
from jax.experimental.pallas import tpu as pltpu
from jax.sharding import Mesh, PartitionSpec as P

HEAD_DIM = 128
HEADS_DEV = 4
TOK = 128
WIDTH = HEADS_DEV * HEAD_DIM
EPSILON = 1e-06
F32 = jnp.float32
BF16 = jnp.bfloat16
CTX = ("y", "zh", "zl")

NN = (((1,), (0,)), ((), ()))
NT = (((1,), (1,)), ((), ()))
TN = (((0,), (0,)), ((), ()))


def mm(a, b, dims):
    return lax.dot_general(a, b, dims, preferred_element_type=F32)


def head(h):
    return slice(h * HEAD_DIM, (h + 1) * HEAD_DIM)


def causal():
    rows = lax.broadcasted_iota(jnp.int32, (TOK, TOK), 0)
    cols = lax.broadcasted_iota(jnp.int32, (TOK, TOK), 1)
    return rows >= cols


def small():
    return pltpu.CompilerParams(vmem_limit_bytes=16 * 1024 * 1024)


def cost(flops, nbytes):
    return pl.CostEstimate(flops=flops, bytes_accessed=nbytes, transcendentals=0)


def blocks_of(value, parity):
    return jnp.concatenate(
        [value[:, 128 * j + 64 * parity : 128 * j + 64 * parity + 64] for j in range(4)], axis=1
    )


def vmem():
    return pl.BlockSpec(memory_space=pltpu.VMEM)


def hbm():
    return pl.BlockSpec(memory_space=pltpu.HBM)


def smem():
    return pl.BlockSpec(memory_space=pltpu.SMEM)


def in_hbm(value):
    return pltpu.with_memory_space_constraint(value, pltpu.HBM)


def state_kernel(k_ref, v_ref, out_ref):
    for h in range(HEADS_DEV):
        out_ref[head(h), :] = mm(k_ref[:, head(h)], v_ref[:, head(h)], TN).astype(BF16)


def local_state(keys, values):
    return pl.pallas_call(
        state_kernel,
        out_shape=jax.ShapeDtypeStruct((WIDTH, HEAD_DIM), BF16),
        compiler_params=small(),
        cost_estimate=cost(2 * TOK * WIDTH * HEAD_DIM, 400000),
        name="local_state",
    )(keys, values)


def split_kernel(place_ref, go_ref, keep_ref, send_ref):
    value = go_ref[...].astype(F32)
    even, odd = blocks_of(value, 0).astype(BF16), blocks_of(value, 1).astype(BF16)
    first = place_ref[0] == 0
    keep_ref[...] = jnp.where(first, even, odd)
    send_ref[...] = jnp.where(first, odd, even)


def split_columns(place, grad_out):
    half = jax.ShapeDtypeStruct((TOK, 256), BF16)
    return pl.pallas_call(
        split_kernel,
        in_specs=[smem(), vmem()],
        out_shape=(half, half),
        compiler_params=small(),
        cost_estimate=cost(TOK * WIDTH, 300000),
        name="split_columns",
    )(place, grad_out)


def scan_kernel(reverse, in_ref, out_ref):
    pairs = in_ref.shape[0] // 16
    total = jnp.zeros((8, HEAD_DIM), F32)
    order = range(pairs - 1, -1, -1) if reverse else range(pairs)
    for i in order:
        rows = slice(16 * i, 16 * i + 16)
        both = in_ref[rows, :].astype(F32)
        low, high = both[:8], both[8:]
        if reverse:
            then = total + high
            out_ref[rows, :] = jnp.concatenate([then, total], axis=0).astype(out_ref.dtype)
            total = then + low
        else:
            then = total + low
            out_ref[rows, :] = jnp.concatenate([total, then], axis=0).astype(out_ref.dtype)
            total = then + high


def exclusive_scan(pieces, reverse):
    return pl.pallas_call(
        functools.partial(scan_kernel, reverse),
        out_shape=jax.ShapeDtypeStruct(pieces.shape, pieces.dtype),
        cost_estimate=cost(WIDTH * HEAD_DIM, 300000),
        compiler_params=small(),
        name="scan_states",
    )(pieces)


def carried(state, reverse):
    pieces = lax.all_to_all(state.reshape(64, 8, HEAD_DIM), CTX, 0, 0)
    sums = exclusive_scan(pieces.reshape(WIDTH, HEAD_DIM), reverse)
    back = lax.all_to_all(sums.reshape(64, 8, HEAD_DIM), CTX, 0, 0)
    return back.reshape(WIDTH, HEAD_DIM)


def attend_kernel(q_ref, k_ref, v_ref, s_ref, pair_ref, normed_ref, scale_ref, p_ref):
    keep = causal()
    for h in range(HEADS_DEV):
        q, k, v = q_ref[:, head(h)], k_ref[:, head(h)], v_ref[:, head(h)]
        weights = jnp.where(keep, mm(q, k, NT), 0.0).astype(BF16)
        p_ref[:, head(h)] = weights
        attended = mm(weights, v, NN) + mm(q, s_ref[head(h), :], NN)
        scale = lax.rsqrt(jnp.mean(attended * attended, axis=-1, keepdims=True) + EPSILON)
        normed = attended * scale
        pair_ref[0, :, head(h)] = normed.astype(BF16)
        pair_ref[1, :, head(h)] = (q.astype(F32) * scale).astype(BF16)
        normed_ref[:, head(h)] = normed
        scale_ref[:, head(h)] = jnp.broadcast_to(scale, (TOK, HEAD_DIM))


def attend(queries, keys, values, before):
    flat = jax.ShapeDtypeStruct((TOK, WIDTH), BF16)
    wide = jax.ShapeDtypeStruct((TOK, WIDTH), F32)
    return pl.pallas_call(
        attend_kernel,
        out_shape=(jax.ShapeDtypeStruct((2, TOK, WIDTH), BF16), wide, wide, flat),
        compiler_params=small(),
        cost_estimate=cost(6 * TOK * WIDTH * HEAD_DIM, 1500000),
        name="attend",
    )(queries, keys, values, before)


def grad_normed_kernel(place_ref, w_ref, go0_ref, go1_ref, go3_ref, go2_ref, far_ref, own_ref, send_ref, w_buf, w_sem):
    x, core = place_ref[1], place_ref[2]
    groups = [2 * lax.rem(x + r, 4) + cs for r in (0, 1, 3, 2) for cs in (core, 1 - core)]
    pieces = [ref.at[i] for ref in (go0_ref, go1_ref, go3_ref) for i in range(2)] + [go2_ref, far_ref]
    loads = [pltpu.make_async_copy(w_ref.at[g], w_buf.at[g], w_sem.at[i]) for i, g in enumerate(groups)]
    for load in loads:
        load.start()
    grad = jnp.zeros((2 * TOK, WIDTH), F32)
    for i in range(8):
        loads[i].wait()
        grad = grad + mm(pieces[i][...].reshape(2 * TOK, 256), w_buf[groups[i]], NN)
    own_ref[...] = grad[:TOK]
    send_ref[...] = grad[TOK:]


def grad_normed_parts(place, weight, grad_parts):
    return pl.pallas_call(
        grad_normed_kernel,
        in_specs=[smem(), hbm()] + [vmem()] * 5,
        out_specs=(vmem(), vmem(), vmem()),
        out_shape=(
            jax.ShapeDtypeStruct((TOK, WIDTH), F32),
            jax.ShapeDtypeStruct((TOK, WIDTH), F32),
            jax.ShapeDtypeStruct((8, 256, WIDTH), BF16),
        ),
        scratch_shapes=[pltpu.SemaphoreType.DMA((8,))],
        compiler_params=small(),
        cost_estimate=cost(2 * TOK * WIDTH * 4096, 4000000),
        name="grad_normed",
    )(place, weight, *grad_parts)


def project_kernel(w_ref, own_ref, other_ref, part_ref, out_buf, out_sem):
    stores = [pltpu.make_async_copy(out_buf.at[g], part_ref.at[g], out_sem.at[g]) for g in range(8)]
    normed = jnp.concatenate([own_ref[0], other_ref[0]], axis=0)
    for g in range(8):
        out_buf[g] = mm(normed, w_ref[g], NT).astype(BF16).reshape(2, TOK, 256)
        stores[g].start()
    for store in stores:
        store.wait()


def project(weight, own, other):
    return pl.pallas_call(
        project_kernel,
        in_specs=[vmem()] * 3,
        out_specs=hbm(),
        out_shape=jax.ShapeDtypeStruct((8, 2, TOK, 256), BF16),
        scratch_shapes=[pltpu.VMEM((8, 2, TOK, 256), BF16), pltpu.SemaphoreType.DMA((8,))],
        compiler_params=small(),
        cost_estimate=cost(2 * TOK * WIDTH * 4096, 4000000),
        name="project",
    )(weight, own, other)


def grad_states_kernel(own_ref, send_ref, normed_ref, scale_ref, q_ref, other_ref, out_ref):
    terms = [], []
    for h in range(HEADS_DEV):
        part, normed = own_ref[:, head(h)], normed_ref[:, head(h)]
        mean = jnp.mean(part * normed, axis=-1, keepdims=True)
        part = (scale_ref[:, head(h)] * (part - normed * mean)).astype(BF16)
        terms[0].append(mm(q_ref[:, head(h)], part, TN))
        part, normed = send_ref[:, head(h)], other_ref[0, :, head(h)].astype(F32)
        mean = jnp.mean(part * normed, axis=-1, keepdims=True)
        part = (part - normed * mean).astype(BF16)
        terms[1].append(mm(other_ref[1, :, head(h)], part, TN))
    own, other = [jnp.concatenate(term, axis=0).reshape(64, 8, HEAD_DIM) for term in terms]
    out_ref[...] = jnp.concatenate([own, other], axis=1).astype(BF16)


def grad_states(own, send, normed, scale, queries, other):
    return pl.pallas_call(
        grad_states_kernel,
        out_shape=jax.ShapeDtypeStruct((64, 16, HEAD_DIM), BF16),
        compiler_params=small(),
        cost_estimate=cost(4 * TOK * WIDTH * HEAD_DIM, 1500000),
        name="grad_states",
    )(own, send, normed, scale, queries, other)


def scan_pairs_kernel(in_ref, out_ref):
    total = jnp.zeros((8, HEAD_DIM), F32)
    for i in range(in_ref.shape[0] // 32 - 1, -1, -1):
        even = in_ref[32 * i : 32 * i + 16, :].astype(F32)
        odd = in_ref[32 * i + 16 : 32 * i + 32, :].astype(F32)
        then = total + (odd[:8] + even[8:])
        out_ref[16 * i : 16 * i + 16, :] = jnp.concatenate([then, total], axis=0).astype(BF16)
        total = then + (even[:8] + odd[8:])


def later_states(states):
    pieces = lax.all_to_all(states, CTX, 0, 0)
    sums = pl.pallas_call(
        scan_pairs_kernel,
        out_shape=jax.ShapeDtypeStruct((WIDTH, HEAD_DIM), BF16),
        compiler_params=small(),
        cost_estimate=cost(2 * WIDTH * HEAD_DIM, 500000),
        name="scan_pairs",
    )(pieces.reshape(2 * WIDTH, HEAD_DIM))
    back = lax.all_to_all(sums.reshape(64, 8, HEAD_DIM), CTX, 0, 0)
    return back.reshape(WIDTH, HEAD_DIM)


def grads_block_kernel(q_ref, k_ref, v_ref, p_ref, own_ref, got_ref, normed_ref, scale_ref, s_ref, gq_ref, gk_ref, gv_ref):
    keep = causal()
    for h in range(HEADS_DEV):
        grad_normed = own_ref[:, head(h)] + got_ref[:, head(h)]
        normed = normed_ref[:, head(h)]
        mean = jnp.mean(grad_normed * normed, axis=-1, keepdims=True)
        ga = (scale_ref[:, head(h)] * (grad_normed - normed * mean)).astype(BF16)
        q, k, v = q_ref[:, head(h)], k_ref[:, head(h)], v_ref[:, head(h)]
        scores = jnp.where(keep, mm(ga, v, NT), 0.0).astype(BF16)
        gq_ref[:, head(h)] = (mm(scores, k, NN) + mm(ga, s_ref[head(h), :], NT)).astype(BF16)
        gk_ref[:, head(h)] = mm(scores, q, TN)
        gv_ref[:, head(h)] = mm(p_ref[:, head(h)], ga, TN)


def grads_block(queries, keys, values, weights, own, got, normed, scale, before):
    flat = jax.ShapeDtypeStruct((TOK, WIDTH), BF16)
    wide = jax.ShapeDtypeStruct((TOK, WIDTH), F32)
    return pl.pallas_call(
        grads_block_kernel,
        out_shape=(flat, wide, wide),
        compiler_params=small(),
        cost_estimate=cost(10 * TOK * WIDTH * HEAD_DIM, 2500000),
        name="grads_block",
    )(queries, keys, values, weights, own, got, normed, scale, before)


def finish_kernel(place_ref, k_ref, v_ref, g_ref, gk_in_ref, gv_in_ref, keep_ref, got_ref, mixed_ref, gk_ref, gv_ref):
    keep, got = keep_ref[...].astype(F32), got_ref[...].astype(F32)
    first = place_ref[0] == 0
    even, odd = jnp.where(first, keep, got), jnp.where(first, got, keep)
    for j in range(4):
        cols = slice(64 * j, 64 * j + 64)
        mixed_ref[:, head(j)] = jnp.concatenate([even[:, cols], odd[:, cols]], axis=1).astype(BF16)
    for h in range(HEADS_DEV):
        after = g_ref[head(h), :]
        gk_ref[:, head(h)] = (gk_in_ref[:, head(h)] + mm(v_ref[:, head(h)], after, NT)).astype(BF16)
        gv_ref[:, head(h)] = (gv_in_ref[:, head(h)] + mm(k_ref[:, head(h)], after, NN)).astype(BF16)


def finish(place, keys, values, after, grad_key, grad_value, keep, got):
    flat = jax.ShapeDtypeStruct((TOK, WIDTH), BF16)
    return pl.pallas_call(
        finish_kernel,
        in_specs=[smem()] + [vmem()] * 7,
        out_shape=(flat, flat, flat),
        compiler_params=small(),
        cost_estimate=cost(4 * TOK * WIDTH * HEAD_DIM, 1500000),
        name="finish",
    )(place, keys, values, after, grad_key, grad_value, keep, got)


def tied(first, second):
    return lax.optimization_barrier((first, second))


SWAP = [(0, 1), (1, 0)]


def repeated(value, times):
    return jnp.broadcast_to(value, (times,) + value.shape)


def shifted(value, axis, step):
    return lax.ppermute(value, axis, [((i + step) % 4, i) for i in range(4)])


def local(queries, keys, values, out_weight, grad_out):
    place = jnp.stack([lax.axis_index(n) for n in ("zl", "x", "core")]).astype(jnp.int32)
    rows = lax.all_to_all(repeated(out_weight.T, 4), "zh", 0, 0)
    grad_keep, grad_send = split_columns(place, in_hbm(grad_out))
    grad_got = lax.ppermute(grad_send, "zl", SWAP)
    state = local_state(in_hbm(keys), in_hbm(values))
    (grad_got, rows), state = tied((grad_got, rows), state)
    grad_pair = jnp.stack([grad_keep, grad_got])
    weight = lax.all_gather(rows, "y").reshape(8, 256, WIDTH)
    weight = in_hbm(weight)
    grad_cores = jnp.stack([grad_pair, lax.ppermute(grad_pair, "core", SWAP)])
    grad_far = shifted(grad_pair, "x", 2)
    grad_parts = [grad_cores] + [shifted(grad_cores, "x", r) for r in (1, 3)]
    grad_parts += [grad_far, lax.ppermute(grad_far, "core", SWAP)]
    before = carried(state, False)
    pair, normed, scale, weights = attend(queries, keys, values, before)
    other = lax.ppermute(pair, "zl", SWAP)
    own, send, weight = grad_normed_parts(place, weight, grad_parts)
    parts = project(weight, pair, other)
    mixed_pair = lax.psum_scatter(parts, ("x", "core"), scatter_dimension=0, tiled=False)
    after = later_states(grad_states(own, send, normed, scale, queries, other))
    got = lax.ppermute(send, "zl", SWAP)
    grad_query, grad_key, grad_value = grads_block(
        queries, keys, values, weights, own, got, normed, scale, before
    )
    mixed_got = lax.ppermute(mixed_pair[1], "zl", SWAP)
    mixed, grad_key, grad_value = finish(
        place, keys, values, after, grad_key, grad_value, mixed_pair[0], mixed_got
    )
    return mixed, grad_query, grad_key, grad_value


def solution(mesh):
    finer = Mesh(mesh.devices.reshape(8, 4, 2, 4, 2), ("y", "zh", "zl", "x", "core"))
    spec = P(CTX, ("x", "core"))
    return jax.shard_map(
        local,
        mesh=finer,
        in_specs=(spec, spec, spec, P(("x", "core"), CTX), spec),
        out_specs=(spec, spec, spec, spec),
        check_vma=False,
    )
```

```python
import functools

import jax
import jax.numpy as jnp
from jax import lax
from jax.experimental import pallas as pl
from jax.experimental.pallas import tpu as pltpu
from jax.sharding import Mesh, PartitionSpec as P

HEAD_DIM = 128
HEADS_DEV = 4
TOK = 128
WIDTH = HEADS_DEV * HEAD_DIM
EPSILON = 1e-06
F32 = jnp.float32
BF16 = jnp.bfloat16
CTX = ("y", "zh", "zl")

NN = (((1,), (0,)), ((), ()))
NT = (((1,), (1,)), ((), ()))
TN = (((0,), (0,)), ((), ()))


def mm(a, b, dims):
    return lax.dot_general(a, b, dims, preferred_element_type=F32)


def head(h):
    return slice(h * HEAD_DIM, (h + 1) * HEAD_DIM)


def causal():
    rows = lax.broadcasted_iota(jnp.int32, (TOK, TOK), 0)
    cols = lax.broadcasted_iota(jnp.int32, (TOK, TOK), 1)
    return rows >= cols


def small():
    return pltpu.CompilerParams(vmem_limit_bytes=16 * 1024 * 1024)


def cost(flops, nbytes):
    return pl.CostEstimate(flops=flops, bytes_accessed=nbytes, transcendentals=0)


def blocks_of(value, parity):
    return jnp.concatenate(
        [value[:, 128 * j + 64 * parity : 128 * j + 64 * parity + 64] for j in range(4)], axis=1
    )


def vmem():
    return pl.BlockSpec(memory_space=pltpu.VMEM)


def hbm():
    return pl.BlockSpec(memory_space=pltpu.HBM)


def smem():
    return pl.BlockSpec(memory_space=pltpu.SMEM)


def in_hbm(value):
    return pltpu.with_memory_space_constraint(value, pltpu.HBM)


def state_kernel(k_ref, v_ref, out_ref):
    for h in range(HEADS_DEV):
        out_ref[head(h), :] = mm(k_ref[:, head(h)], v_ref[:, head(h)], TN).astype(BF16)


def local_state(keys, values):
    return pl.pallas_call(
        state_kernel,
        out_shape=jax.ShapeDtypeStruct((WIDTH, HEAD_DIM), BF16),
        compiler_params=small(),
        cost_estimate=cost(2 * TOK * WIDTH * HEAD_DIM, 400000),
        name="local_state",
    )(keys, values)


def split_kernel(place_ref, go_ref, keep_ref, send_ref):
    value = go_ref[...].astype(F32)
    even, odd = blocks_of(value, 0).astype(BF16), blocks_of(value, 1).astype(BF16)
    first = place_ref[0] == 0
    keep_ref[...] = jnp.where(first, even, odd)
    send_ref[...] = jnp.where(first, odd, even)


def split_columns(place, grad_out):
    half = jax.ShapeDtypeStruct((TOK, 256), BF16)
    return pl.pallas_call(
        split_kernel,
        in_specs=[smem(), vmem()],
        out_shape=(half, half),
        compiler_params=small(),
        cost_estimate=cost(TOK * WIDTH, 300000),
        name="split_columns",
    )(place, grad_out)


def scan_kernel(reverse, in_ref, out_ref):
    pairs = in_ref.shape[0] // 16
    total = jnp.zeros((8, HEAD_DIM), F32)
    order = range(pairs - 1, -1, -1) if reverse else range(pairs)
    for i in order:
        rows = slice(16 * i, 16 * i + 16)
        both = in_ref[rows, :].astype(F32)
        low, high = both[:8], both[8:]
        if reverse:
            then = total + high
            out_ref[rows, :] = jnp.concatenate([then, total], axis=0).astype(out_ref.dtype)
            total = then + low
        else:
            then = total + low
            out_ref[rows, :] = jnp.concatenate([total, then], axis=0).astype(out_ref.dtype)
            total = then + high


def exclusive_scan(pieces, reverse):
    return pl.pallas_call(
        functools.partial(scan_kernel, reverse),
        out_shape=jax.ShapeDtypeStruct(pieces.shape, pieces.dtype),
        cost_estimate=cost(WIDTH * HEAD_DIM, 300000),
        compiler_params=small(),
        name="scan_states",
    )(pieces)


def carried(state, reverse):
    pieces = lax.all_to_all(state.reshape(64, 8, HEAD_DIM), CTX, 0, 0)
    sums = exclusive_scan(pieces.reshape(WIDTH, HEAD_DIM), reverse)
    back = lax.all_to_all(sums.reshape(64, 8, HEAD_DIM), CTX, 0, 0)
    return back.reshape(WIDTH, HEAD_DIM)


def attend_kernel(q_ref, k_ref, v_ref, s_ref, pair_ref, normed_ref, scale_ref, p_ref):
    keep = causal()
    for h in range(HEADS_DEV):
        q, k, v = q_ref[:, head(h)], k_ref[:, head(h)], v_ref[:, head(h)]
        weights = jnp.where(keep, mm(q, k, NT), 0.0).astype(BF16)
        p_ref[:, head(h)] = weights
        attended = mm(weights, v, NN) + mm(q, s_ref[head(h), :], NN)
        scale = lax.rsqrt(jnp.mean(attended * attended, axis=-1, keepdims=True) + EPSILON)
        normed = attended * scale
        pair_ref[0, :, head(h)] = normed.astype(BF16)
        pair_ref[1, :, head(h)] = (q.astype(F32) * scale).astype(BF16)
        normed_ref[:, head(h)] = normed
        scale_ref[:, head(h)] = jnp.broadcast_to(scale, (TOK, HEAD_DIM))


def attend(queries, keys, values, before):
    flat = jax.ShapeDtypeStruct((TOK, WIDTH), BF16)
    wide = jax.ShapeDtypeStruct((TOK, WIDTH), F32)
    return pl.pallas_call(
        attend_kernel,
        out_shape=(jax.ShapeDtypeStruct((2, TOK, WIDTH), BF16), wide, wide, flat),
        compiler_params=small(),
        cost_estimate=cost(6 * TOK * WIDTH * HEAD_DIM, 1500000),
        name="attend",
    )(queries, keys, values, before)


def grad_normed_kernel(place_ref, w_ref, go0_ref, go1_ref, go3_ref, go2_ref, far_ref, own_ref, send_ref, w_buf, w_sem):
    x, core = place_ref[1], place_ref[2]
    groups = [2 * lax.rem(x + r, 4) + cs for r in (0, 1, 3, 2) for cs in (core, 1 - core)]
    pieces = [ref.at[i] for ref in (go0_ref, go1_ref, go3_ref) for i in range(2)] + [go2_ref, far_ref]
    loads = [pltpu.make_async_copy(w_ref.at[g], w_buf.at[g], w_sem.at[i]) for i, g in enumerate(groups)]
    for load in loads:
        load.start()
    grad = jnp.zeros((2 * TOK, WIDTH), F32)
    for i in range(8):
        loads[i].wait()
        grad = grad + mm(pieces[i][...].reshape(2 * TOK, 256), w_buf[groups[i]], NN)
    own_ref[...] = grad[:TOK]
    send_ref[...] = grad[TOK:]


def grad_normed_parts(place, weight, grad_parts):
    return pl.pallas_call(
        grad_normed_kernel,
        in_specs=[smem(), hbm()] + [vmem()] * 5,
        out_specs=(vmem(), vmem(), vmem()),
        out_shape=(
            jax.ShapeDtypeStruct((TOK, WIDTH), F32),
            jax.ShapeDtypeStruct((TOK, WIDTH), F32),
            jax.ShapeDtypeStruct((8, 256, WIDTH), BF16),
        ),
        scratch_shapes=[pltpu.SemaphoreType.DMA((8,))],
        compiler_params=small(),
        cost_estimate=cost(2 * TOK * WIDTH * 4096, 4000000),
        name="grad_normed",
    )(place, weight, *grad_parts)


def project_kernel(w_ref, own_ref, other_ref, part_ref, out_buf, out_sem):
    stores = [pltpu.make_async_copy(out_buf.at[g], part_ref.at[g], out_sem.at[g]) for g in range(8)]
    normed = jnp.concatenate([own_ref[0], other_ref[0]], axis=0)
    for g in range(8):
        out_buf[g] = mm(normed, w_ref[g], NT).astype(BF16).reshape(2, TOK, 256)
        stores[g].start()
    for store in stores:
        store.wait()


def project(weight, own, other):
    return pl.pallas_call(
        project_kernel,
        in_specs=[vmem()] * 3,
        out_specs=hbm(),
        out_shape=jax.ShapeDtypeStruct((8, 2, TOK, 256), BF16),
        scratch_shapes=[pltpu.VMEM((8, 2, TOK, 256), BF16), pltpu.SemaphoreType.DMA((8,))],
        compiler_params=small(),
        cost_estimate=cost(2 * TOK * WIDTH * 4096, 4000000),
        name="project",
    )(weight, own, other)


def grad_states_kernel(own_ref, send_ref, normed_ref, scale_ref, q_ref, other_ref, out_ref):
    terms = [], []
    for h in range(HEADS_DEV):
        part, normed = own_ref[:, head(h)], normed_ref[:, head(h)]
        mean = jnp.mean(part * normed, axis=-1, keepdims=True)
        part = (scale_ref[:, head(h)] * (part - normed * mean)).astype(BF16)
        terms[0].append(mm(q_ref[:, head(h)], part, TN))
        part, normed = send_ref[:, head(h)], other_ref[0, :, head(h)].astype(F32)
        mean = jnp.mean(part * normed, axis=-1, keepdims=True)
        part = (part - normed * mean).astype(BF16)
        terms[1].append(mm(other_ref[1, :, head(h)], part, TN))
    own, other = [jnp.concatenate(term, axis=0).reshape(64, 8, HEAD_DIM) for term in terms]
    out_ref[...] = jnp.concatenate([own, other], axis=1).astype(BF16)


def grad_states(own, send, normed, scale, queries, other):
    return pl.pallas_call(
        grad_states_kernel,
        out_shape=jax.ShapeDtypeStruct((64, 16, HEAD_DIM), BF16),
        compiler_params=small(),
        cost_estimate=cost(4 * TOK * WIDTH * HEAD_DIM, 1500000),
        name="grad_states",
    )(own, send, normed, scale, queries, other)


def scan_pairs_kernel(in_ref, out_ref):
    total = jnp.zeros((8, HEAD_DIM), F32)
    for i in range(in_ref.shape[0] // 32 - 1, -1, -1):
        even = in_ref[32 * i : 32 * i + 16, :].astype(F32)
        odd = in_ref[32 * i + 16 : 32 * i + 32, :].astype(F32)
        then = total + (odd[:8] + even[8:])
        out_ref[16 * i : 16 * i + 16, :] = jnp.concatenate([then, total], axis=0).astype(BF16)
        total = then + (even[:8] + odd[8:])


def later_states(states):
    pieces = lax.all_to_all(states, CTX, 0, 0)
    sums = pl.pallas_call(
        scan_pairs_kernel,
        out_shape=jax.ShapeDtypeStruct((WIDTH, HEAD_DIM), BF16),
        compiler_params=small(),
        cost_estimate=cost(2 * WIDTH * HEAD_DIM, 500000),
        name="scan_pairs",
    )(pieces.reshape(2 * WIDTH, HEAD_DIM))
    back = lax.all_to_all(sums.reshape(64, 8, HEAD_DIM), CTX, 0, 0)
    return back.reshape(WIDTH, HEAD_DIM)


def grads_block_kernel(q_ref, k_ref, v_ref, p_ref, own_ref, got_ref, normed_ref, scale_ref, s_ref, gq_ref, gk_ref, gv_ref):
    keep = causal()
    for h in range(HEADS_DEV):
        grad_normed = own_ref[:, head(h)] + got_ref[:, head(h)]
        normed = normed_ref[:, head(h)]
        mean = jnp.mean(grad_normed * normed, axis=-1, keepdims=True)
        ga = (scale_ref[:, head(h)] * (grad_normed - normed * mean)).astype(BF16)
        q, k, v = q_ref[:, head(h)], k_ref[:, head(h)], v_ref[:, head(h)]
        scores = jnp.where(keep, mm(ga, v, NT), 0.0).astype(BF16)
        gq_ref[:, head(h)] = (mm(scores, k, NN) + mm(ga, s_ref[head(h), :], NT)).astype(BF16)
        gk_ref[:, head(h)] = mm(scores, q, TN)
        gv_ref[:, head(h)] = mm(p_ref[:, head(h)], ga, TN)


def grads_block(queries, keys, values, weights, own, got, normed, scale, before):
    flat = jax.ShapeDtypeStruct((TOK, WIDTH), BF16)
    wide = jax.ShapeDtypeStruct((TOK, WIDTH), F32)
    return pl.pallas_call(
        grads_block_kernel,
        out_shape=(flat, wide, wide),
        compiler_params=small(),
        cost_estimate=cost(10 * TOK * WIDTH * HEAD_DIM, 2500000),
        name="grads_block",
    )(queries, keys, values, weights, own, got, normed, scale, before)


def finish_kernel(place_ref, k_ref, v_ref, g_ref, gk_in_ref, gv_in_ref, keep_ref, got_ref, mixed_ref, gk_ref, gv_ref):
    keep, got = keep_ref[...].astype(F32), got_ref[...].astype(F32)
    first = place_ref[0] == 0
    even, odd = jnp.where(first, keep, got), jnp.where(first, got, keep)
    for j in range(4):
        cols = slice(64 * j, 64 * j + 64)
        mixed_ref[:, head(j)] = jnp.concatenate([even[:, cols], odd[:, cols]], axis=1).astype(BF16)
    for h in range(HEADS_DEV):
        after = g_ref[head(h), :]
        gk_ref[:, head(h)] = (gk_in_ref[:, head(h)] + mm(v_ref[:, head(h)], after, NT)).astype(BF16)
        gv_ref[:, head(h)] = (gv_in_ref[:, head(h)] + mm(k_ref[:, head(h)], after, NN)).astype(BF16)


def finish(place, keys, values, after, grad_key, grad_value, keep, got):
    flat = jax.ShapeDtypeStruct((TOK, WIDTH), BF16)
    return pl.pallas_call(
        finish_kernel,
        in_specs=[smem()] + [vmem()] * 7,
        out_shape=(flat, flat, flat),
        compiler_params=small(),
        cost_estimate=cost(4 * TOK * WIDTH * HEAD_DIM, 1500000),
        name="finish",
    )(place, keys, values, after, grad_key, grad_value, keep, got)


def tied(first, second):
    return lax.optimization_barrier((first, second))


SWAP = [(0, 1), (1, 0)]


def repeated(value, times):
    return jnp.broadcast_to(value, (times,) + value.shape)


def shifted(value, axis, step):
    return lax.ppermute(value, axis, [((i + step) % 4, i) for i in range(4)])


def local(queries, keys, values, out_weight, grad_out):
    place = jnp.stack([lax.axis_index(n) for n in ("zl", "x", "core")]).astype(jnp.int32)
    rows = lax.all_to_all(repeated(out_weight.T, 4), "zh", 0, 0)
    grad_keep, grad_send = split_columns(place, in_hbm(grad_out))
    grad_got = lax.ppermute(grad_send, "zl", SWAP)
    state = local_state(in_hbm(keys), in_hbm(values))
    (grad_got, rows), state = tied((grad_got, rows), state)
    grad_pair = jnp.stack([grad_keep, grad_got])
    weight = lax.all_gather(rows, "y").reshape(8, 256, WIDTH)
    weight = in_hbm(weight)
    grad_cores = jnp.stack([grad_pair, lax.ppermute(grad_pair, "core", SWAP)])
    grad_far = shifted(grad_pair, "x", 2)
    grad_parts = [grad_cores] + [shifted(grad_cores, "x", r) for r in (1, 3)]
    grad_parts += [grad_far, lax.ppermute(grad_far, "core", SWAP)]
    before = carried(state, False)
    pair, normed, scale, weights = attend(queries, keys, values, before)
    pair, grad_parts[-1] = tied(pair, grad_parts[-1])
    other = lax.ppermute(pair, "zl", SWAP)
    own, send, weight = grad_normed_parts(place, weight, grad_parts)
    parts = project(weight, pair, other)
    mixed_pair = lax.psum_scatter(parts, ("x", "core"), scatter_dimension=0, tiled=False)
    after = later_states(grad_states(own, send, normed, scale, queries, other))
    got = lax.ppermute(send, "zl", SWAP)
    grad_query, grad_key, grad_value = grads_block(
        queries, keys, values, weights, own, got, normed, scale, before
    )
    mixed_got = lax.ppermute(mixed_pair[1], "zl", SWAP)
    mixed, grad_key, grad_value = finish(
        place, keys, values, after, grad_key, grad_value, mixed_pair[0], mixed_got
    )
    return mixed, grad_query, grad_key, grad_value


def solution(mesh):
    finer = Mesh(mesh.devices.reshape(8, 4, 2, 4, 2), ("y", "zh", "zl", "x", "core"))
    spec = P(CTX, ("x", "core"))
    return jax.shard_map(
        local,
        mesh=finer,
        in_specs=(spec, spec, spec, P(("x", "core"), CTX), spec),
        out_specs=(spec, spec, spec, spec),
        check_vma=False,
    )
```
